512 devices in a mesh: grp: 16 (over z_lo, x), dev: 32 (over y, z_hi, core).
Axes of the slice: x: 4, y: 8, z: 8 (z_hi: 2, z_lo: 4; z = z_hi * 4 + z_lo), core: 2. Of those that a mesh axis runs over, the one named last changes fastest.
Arguments:
- coeffs: bfloat16 [32768, 1024], P(('grp', 'dev')), may hold values from -6 to 6
- self_blocks: bfloat16 [4, 32768, 1024], P(None, 'grp'), may hold values from -0.75 to 0.75
- cross_blocks: bfloat16 [4, 32768, 1024], P(None, 'grp'), may hold values from -0.75 to 0.75
- pattern: int32 [4, 512, 64], P(None, 'grp'), may hold values from 0 to 63, each once within a row
Outputs:
- result: bfloat16 [32768, 1024], P(('grp', 'dev'))
The draws below stay inside these ranges and needn't reach their ends.
Inputs may be any that keep to these rules, and one draw needn't show every extreme that they name: Each row pattern[l, p, :] is a permutation of the local box indices.
All inputs are finite; a program needn't handle non-finite values.
Results may differ from the reference program's by a relative error of at most 0.0064.
Values may be sent and summed in bfloat16 or wider, within the bound.
A program may use at most 128 MiB of HBM per device.

```python
import jax
import jax.numpy as jnp

R = 32
K = 32
BOX_DEV = 64
LEVELS = 4
DEVICES_ALL = 512
BOXES = 32768
N_GRP = 16
N_DEV = 32


def steps_of(stream_key, shape, pieces, low, top_value):
    def one(position, blocks):
        heights = jax.random.uniform(jax.random.fold_in(jax.random.fold_in(stream_key, 6), position), (blocks,), jnp.float32, low / len(pieces), top_value / len(pieces))
        return jnp.repeat(jnp.exp(heights), shape[position] // blocks).reshape((-1,) + (1,) * (len(shape) - position - 1))

    loudness = one(*pieces[0])
    for cut in pieces[1:]:
        loudness = loudness * one(*cut)
    return loudness


def gaussian(stream_key, extent, scale, most, shards=(), kind=jnp.bfloat16):
    drawn = jax.random.normal(stream_key, extent, jnp.float32) * scale
    if len(shards) > 0:
        drawn = steps_of(stream_key, extent, shards, -0.22, 0.18) * drawn
    return jnp.clip(drawn, min=-most, max=most).astype(kind)


def setup_inputs(seed: int = 0) -> dict:
    arg_keys = jax.random.split(jax.random.key(seed), 5)
    return {
        "coeffs": gaussian(arg_keys[0], (BOXES, K * R), 1.0, 6.0, ((0, 512),)),
        "self_blocks": gaussian(arg_keys[1], (LEVELS, BOXES, R * R), (2 * R) ** -0.5, 0.75, ((1, 16),)),
        "cross_blocks": gaussian(arg_keys[2], (LEVELS, BOXES, R * R), (2 * R) ** -0.5, 0.75, ((1, 16),)),
        "pattern": jax.vmap(lambda own: jax.random.permutation(own, BOX_DEV))(jax.random.split(arg_keys[3], LEVELS * DEVICES_ALL)).reshape((LEVELS, DEVICES_ALL, BOX_DEV)).astype(jnp.int32),
    }


def level_step(state, self_w, cross_w, order, mask):
    count = state.shape[0]
    partner = state[jnp.arange(count, dtype=jnp.int32) ^ mask]
    picked = jnp.take_along_axis(partner, order.astype(jnp.int32)[:, :, None, None], axis=1)
    own_term = jnp.einsum('pbkr,pbsr->pbks', state.astype(jnp.float32), self_w.astype(jnp.float32))
    cross_term = jnp.einsum('pbkr,pbsr->pbks', picked.astype(jnp.float32), cross_w.astype(jnp.float32))
    return (own_term + cross_term).astype(jnp.bfloat16)


def reference(coeffs, self_blocks, cross_blocks, pattern):
    count = N_GRP * N_DEV
    masks = [N_DEV // 2, 1, (N_GRP // 2) * N_DEV, N_DEV]
    state = coeffs.reshape(count, BOX_DEV, K, R)
    for level in range(LEVELS):
        self_w = self_blocks[level].reshape(count, BOX_DEV, R, R)
        cross_w = cross_blocks[level].reshape(count, BOX_DEV, R, R)
        state = level_step(state, self_w, cross_w, pattern[level], masks[level])
    return state.reshape(count * BOX_DEV, K * R)
```

```python
import functools

import jax
import jax.numpy as jnp
from jax import lax
from jax.experimental import pallas as pl
from jax.experimental.pallas import tpu as pltpu
from jax.sharding import PartitionSpec as P

R = 32
LEVELS = 4
CHUNKS = 4
ROWS = 128
MESH = pl.DeviceIdType.MESH


def iota(shape, dim):
    return lax.broadcasted_iota(jnp.int32, shape, dim)


def order_of_stages():
    offset = (0.0, 1.25, 3.85, 5.95)
    stages = [(offset[l] + 0.75 * c, l, c) for l in range(LEVELS) for c in range(CHUNKS)]
    return [(l, c) for _, l, c in sorted(stages)]


def kernel(
    n_grp, n_dev, x_hbm, self_hbm, cross_hbm, pat_hbm, o_ref,
    pat_ref, xn, wn, w, q, xs, xp, part, send, near, got, send_sem, recv_sem, load_sem,
):
    grp = lax.axis_index("grp")
    dev = lax.axis_index("dev")
    boxes = xn.shape[0]
    partner = (
        (grp, dev ^ (n_dev // 2)),
        (grp, dev ^ 1),
        (grp ^ (n_grp // 2), dev),
        (grp ^ 1, dev),
    )
    barrier = pltpu.get_barrier_semaphore()
    for level in range(LEVELS):
        pl.semaphore_signal(barrier, inc=1, device_id=partner[level], device_id_type=MESH)

    row0 = pl.multiple_of(dev * boxes, boxes)
    load_x = pltpu.make_async_copy(x_hbm, xn, load_sem.at[2 * LEVELS])
    load_x.start()
    load_pat = pltpu.make_async_copy(pat_hbm, pat_ref, load_sem.at[2 * LEVELS + 1])
    load_pat.start()
    loads = []
    for level in range(LEVELS):
        pair = []
        for kind, src in enumerate((self_hbm, cross_hbm)):
            copy = pltpu.make_async_copy(
                src.at[level, pl.ds(row0, boxes)], wn.at[level, kind], load_sem.at[2 * level + kind]
            )
            copy.start()
            pair.append(copy)
        loads.append(pair)

    load_pat.wait()
    for level in range(LEVELS):
        row = pat_ref[level, pl.ds(dev, 1), :]
        row = jnp.concatenate([row, row + boxes], axis=1)
        q[level] = (iota((ROWS, ROWS), 0) == row).astype(jnp.float32).astype(jnp.bfloat16)

    turned = iota((256, 256), 0)
    pick = ((turned % 8) * R + turned // 8 == iota((256, 256), 1)).astype(jnp.float32).astype(jnp.bfloat16)

    def prepare(level):
        for copy in loads[level]:
            copy.wait()
        for t in range(4):
            own = wn[level, 0, :, t * 256:(t + 1) * 256]
            other = wn[level, 1, :, t * 256:(t + 1) * 256]
            stack = jnp.concatenate([own, own, other, other], axis=0)
            out = lax.dot_general(
                pick, stack, (((1,), (1,)), ((), ())), preferred_element_type=jnp.float32
            )
            w[level, 0, t] = out[:, :ROWS]
            w[level, 1, t] = out[:, ROWS:]

    def stacked(ref, c):
        return jnp.concatenate(
            [ref[:, c * 256:c * 256 + 128], ref[:, c * 256 + 128:c * 256 + 256]], axis=0
        )

    def apply(level, kind, ref, accs):
        def step(r, accs):
            ws = [w[level, kind, t, pl.ds(pl.multiple_of(r * 8, 8), 8), :] for t in range(4)]
            out = []
            for k in range(4):
                x = ref[pl.ds(k * R + r, 1), :]
                out += [accs[4 * k + t] + ws[t] * x for t in range(4)]
            return tuple(out)

        return lax.fori_loop(0, R, step, tuple(accs), unroll=8)

    def self_stage(level, c):
        zero = jnp.zeros((8, ROWS), jnp.float32)
        accs = apply(level, 0, xs.at[level, c], [zero] * 16)
        for i in range(16):
            part[level, c, i * 8:(i + 1) * 8, :] = accs[i]

    def exchange(level, c):
        if level == 0:
            src = xn.at[:, pl.ds(c * 256, 256)]
            dst = near.at[:, pl.ds(c * 256, 256)]
        else:
            src = send.at[level - 1, c]
            dst = got.at[level - 1, c]
        return pltpu.make_async_remote_copy(
            src_ref=src, dst_ref=dst,
            send_sem=send_sem.at[level, c], recv_sem=recv_sem.at[level, c],
            device_id=partner[level], device_id_type=MESH,
        )

    def cross_stage(level, c):
        exchange(level, c).wait_recv()
        if level == 0:
            xp[...] = lax.dot_general(
                stacked(near, c), q[0], (((0,), (0,)), ((), ())), preferred_element_type=jnp.float32
            )
        else:
            xp[...] = jnp.dot(got[level - 1, c], q[level], preferred_element_type=jnp.float32)
        accs = apply(level, 1, xp, [part[level, c, i * 8:(i + 1) * 8, :] for i in range(16)])
        total = jnp.concatenate(accs, axis=0)
        if level < LEVELS - 1:
            total = total.astype(jnp.bfloat16)
            send[level, c] = total
            exchange(level + 1, c).start()
            xs[level + 1, c] = total.astype(jnp.float32)
            self_stage(level + 1, c)
        else:
            total = total.T.astype(jnp.bfloat16)
            o_ref[:, c * 256:c * 256 + 128] = total[:boxes]
            o_ref[:, c * 256 + 128:c * 256 + 256] = total[boxes:]

    load_x.wait()
    prepare(0)
    for c in range(CHUNKS):
        xs[0, c] = stacked(xn, c).astype(jnp.float32).T
    pl.semaphore_wait(barrier, LEVELS)
    for c in range(CHUNKS):
        exchange(0, c).start()
    for c in range(CHUNKS):
        self_stage(0, c)
    for level in range(1, LEVELS):
        prepare(level)
    for level, c in order_of_stages():
        cross_stage(level, c)
    for level in range(LEVELS):
        for c in range(CHUNKS):
            exchange(level, c).wait_send()


def shards(n_grp, n_dev, coeffs, self_blocks, cross_blocks, pattern):
    boxes, width = coeffs.shape
    bf16, f32 = jnp.bfloat16, jnp.float32
    hbm = pl.BlockSpec(memory_space=pltpu.HBM)
    vmem = pl.BlockSpec(memory_space=pltpu.VMEM)
    return pl.pallas_call(
        functools.partial(kernel, n_grp, n_dev),
        out_shape=jax.ShapeDtypeStruct((boxes, width), bf16),
        in_specs=[hbm, hbm, hbm, hbm],
        out_specs=vmem,
        scratch_shapes=[
            pltpu.VMEM(pattern.shape, jnp.int32),
            pltpu.VMEM((boxes, width), bf16),
            pltpu.VMEM((LEVELS, 2, boxes, width), bf16),
            pltpu.VMEM((LEVELS, 2, 4, 256, ROWS), f32),
            pltpu.VMEM((LEVELS, ROWS, ROWS), bf16),
            pltpu.VMEM((LEVELS, CHUNKS, ROWS, ROWS), f32),
            pltpu.VMEM((ROWS, ROWS), f32),
            pltpu.VMEM((LEVELS, CHUNKS, ROWS, ROWS), f32),
            pltpu.VMEM((LEVELS - 1, CHUNKS, ROWS, ROWS), bf16),
            pltpu.VMEM((boxes, width), bf16),
            pltpu.VMEM((LEVELS - 1, CHUNKS, ROWS, ROWS), bf16),
            pltpu.SemaphoreType.DMA((LEVELS, CHUNKS)),
            pltpu.SemaphoreType.DMA((LEVELS, CHUNKS)),
            pltpu.SemaphoreType.DMA((2 * LEVELS + 2,)),
        ],
        compiler_params=pltpu.CompilerParams(
            collective_id=0, has_side_effects=True, vmem_limit_bytes=60 * 2**20
        ),
        name="butterfly",
    )(coeffs, self_blocks, cross_blocks, pattern)


def solution(mesh):
    return jax.shard_map(
        functools.partial(shards, mesh.shape["grp"], mesh.shape["dev"]),
        mesh=mesh,
        in_specs=(
            P(("grp", "dev"), None),
            P(None, "grp", None),
            P(None, "grp", None),
            P(None, "grp", None),
        ),
        out_specs=P(("grp", "dev"), None),
        check_vma=False,
    )
```

```python
import functools

import jax
import jax.numpy as jnp
from jax import lax
from jax.experimental import pallas as pl
from jax.experimental.pallas import tpu as pltpu
from jax.sharding import PartitionSpec as P

R = 32
LEVELS = 4
CHUNKS = 4
ROWS = 128
MESH = pl.DeviceIdType.MESH


def iota(shape, dim):
    return lax.broadcasted_iota(jnp.int32, shape, dim)


def order_of_stages():
    first = [(0, 0)] + [p for c in range(1, CHUNKS) for p in ((0, c), (1, c - 1))] + [(1, CHUNKS - 1)]
    return first + [(l, c) for l in (2, 3) for c in range(CHUNKS)]


def kernel(
    n_grp, n_dev, x_hbm, self_hbm, cross_hbm, pat_hbm, o_ref,
    pat_ref, xn, wn, w, q, xs, xp, part, send, near, got, send_sem, recv_sem, load_sem,
):
    grp = lax.axis_index("grp")
    dev = lax.axis_index("dev")
    boxes = xn.shape[0]
    partner = (
        (grp, dev ^ (n_dev // 2)),
        (grp, dev ^ 1),
        (grp ^ (n_grp // 2), dev),
        (grp ^ 1, dev),
    )
    barrier = pltpu.get_barrier_semaphore()
    for level in range(LEVELS):
        pl.semaphore_signal(barrier, inc=1, device_id=partner[level], device_id_type=MESH)

    row0 = pl.multiple_of(dev * boxes, boxes)
    load_x = pltpu.make_async_copy(x_hbm, xn, load_sem.at[2 * LEVELS])
    load_x.start()
    load_pat = pltpu.make_async_copy(pat_hbm, pat_ref, load_sem.at[2 * LEVELS + 1])
    load_pat.start()
    loads = []
    for level in range(LEVELS):
        pair = []
        for kind, src in enumerate((self_hbm, cross_hbm)):
            copy = pltpu.make_async_copy(
                src.at[level, pl.ds(row0, boxes)], wn.at[level, kind], load_sem.at[2 * level + kind]
            )
            copy.start()
            pair.append(copy)
        loads.append(pair)

    def exchange(level, c):
        if level == 0:
            src = xn.at[:, pl.ds(c * 256, 256)]
            dst = near.at[:, pl.ds(c * 256, 256)]
        else:
            src = send.at[level - 1, c]
            dst = got.at[level - 1, c]
        return pltpu.make_async_remote_copy(
            src_ref=src, dst_ref=dst,
            send_sem=send_sem.at[level, c], recv_sem=recv_sem.at[level, c],
            device_id=partner[level], device_id_type=MESH,
        )

    load_x.wait()
    pl.semaphore_wait(barrier, LEVELS)
    for c in range(CHUNKS):
        exchange(0, c).start()

    load_pat.wait()
    for level in range(LEVELS):
        row = pat_ref[level, pl.ds(dev, 1), :]
        row = jnp.concatenate([row, row + boxes], axis=1)
        q[level] = (iota((ROWS, ROWS), 0) == row).astype(jnp.float32).astype(jnp.bfloat16)

    turned = iota((256, 256), 0)
    pick = ((turned % 8) * R + turned // 8 == iota((256, 256), 1)).astype(jnp.float32).astype(jnp.bfloat16)

    def prepare(level):
        for copy in loads[level]:
            copy.wait()
        for t in range(4):
            own = wn[level, 0, :, t * 256:(t + 1) * 256]
            other = wn[level, 1, :, t * 256:(t + 1) * 256]
            stack = jnp.concatenate([own, own, other, other], axis=0)
            out = lax.dot_general(
                pick, stack, (((1,), (1,)), ((), ())), preferred_element_type=jnp.float32
            )
            w[level, 0, t] = out[:, :ROWS]
            w[level, 1, t] = out[:, ROWS:]

    def stacked(ref, c):
        return jnp.concatenate(
            [ref[:, c * 256:c * 256 + 128], ref[:, c * 256 + 128:c * 256 + 256]], axis=0
        )

    def apply(level, kind, ref, accs):
        def step(r, accs):
            ws = [w[level, kind, t, pl.ds(pl.multiple_of(r * 8, 8), 8), :] for t in range(4)]
            out = []
            for k in range(4):
                x = ref[pl.ds(k * R + r, 1), :]
                out += [accs[4 * k + t] + ws[t] * x for t in range(4)]
            return tuple(out)

        return lax.fori_loop(0, R, step, tuple(accs), unroll=32)

    def self_stage(level, c):
        zero = jnp.zeros((8, ROWS), jnp.float32)
        accs = apply(level, 0, xs.at[level, c], [zero] * 16)
        for i in range(16):
            part[level, c, i * 8:(i + 1) * 8, :] = accs[i]

    def cross_stage(level, c):
        if level == 2:
            self_stage(2, c)
        exchange(level, c).wait_recv()
        if level == 0:
            xp[...] = lax.dot_general(
                stacked(near, c), q[0], (((0,), (0,)), ((), ())), preferred_element_type=jnp.float32
            )
        else:
            xp[...] = jnp.dot(got[level - 1, c], q[level], preferred_element_type=jnp.float32)
        accs = apply(level, 1, xp, [part[level, c, i * 8:(i + 1) * 8, :] for i in range(16)])
        total = jnp.concatenate(accs, axis=0)
        if level < LEVELS - 1:
            total = total.astype(jnp.bfloat16)
            send[level, c] = total
            exchange(level + 1, c).start()
            xs[level + 1, c] = total.astype(jnp.float32)
            if level != 1:
                self_stage(level + 1, c)
        else:
            total = total.T.astype(jnp.bfloat16)
            o_ref[:, c * 256:c * 256 + 128] = total[:boxes]
            o_ref[:, c * 256 + 128:c * 256 + 256] = total[boxes:]

    prepare(0)
    for c in range(CHUNKS):
        xs[0, c] = stacked(xn, c).astype(jnp.float32).T
    for c in range(CHUNKS):
        self_stage(0, c)
    for level in range(1, LEVELS):
        prepare(level)
    for level, c in order_of_stages():
        cross_stage(level, c)
    for level in range(LEVELS):
        for c in range(CHUNKS):
            exchange(level, c).wait_send()


def shards(n_grp, n_dev, coeffs, self_blocks, cross_blocks, pattern):
    boxes, width = coeffs.shape
    bf16, f32 = jnp.bfloat16, jnp.float32
    hbm = pl.BlockSpec(memory_space=pltpu.HBM)
    vmem = pl.BlockSpec(memory_space=pltpu.VMEM)
    return pl.pallas_call(
        functools.partial(kernel, n_grp, n_dev),
        out_shape=pltpu.VMEM((boxes, width), bf16),
        in_specs=[hbm, hbm, hbm, hbm],
        out_specs=vmem,
        scratch_shapes=[
            pltpu.VMEM(pattern.shape, jnp.int32),
            pltpu.VMEM((boxes, width), bf16),
            pltpu.VMEM((LEVELS, 2, boxes, width), bf16),
            pltpu.VMEM((LEVELS, 2, 4, 256, ROWS), f32),
            pltpu.VMEM((LEVELS, ROWS, ROWS), bf16),
            pltpu.VMEM((LEVELS, CHUNKS, ROWS, ROWS), f32),
            pltpu.VMEM((ROWS, ROWS), f32),
            pltpu.VMEM((LEVELS, CHUNKS, ROWS, ROWS), f32),
            pltpu.VMEM((LEVELS - 1, CHUNKS, ROWS, ROWS), bf16),
            pltpu.VMEM((boxes, width), bf16),
            pltpu.VMEM((LEVELS - 1, CHUNKS, ROWS, ROWS), bf16),
            pltpu.SemaphoreType.DMA((LEVELS, CHUNKS)),
            pltpu.SemaphoreType.DMA((LEVELS, CHUNKS)),
            pltpu.SemaphoreType.DMA((2 * LEVELS + 2,)),
        ],
        compiler_params=pltpu.CompilerParams(
            collective_id=0, has_side_effects=True, vmem_limit_bytes=60 * 2**20
        ),
        name="butterfly",
    )(coeffs, self_blocks, cross_blocks, pattern)


def solution(mesh):
    return jax.shard_map(
        functools.partial(shards, mesh.shape["grp"], mesh.shape["dev"]),
        mesh=mesh,
        in_specs=(
            P(("grp", "dev"), None),
            P(None, "grp", None),
            P(None, "grp", None),
            P(None, "grp", None),
        ),
        out_specs=P(("grp", "dev"), None),
        check_vma=False,
    )
```

```python
import functools

import jax
import jax.numpy as jnp
from jax import lax
from jax.experimental import pallas as pl
from jax.experimental.pallas import tpu as pltpu
from jax.sharding import PartitionSpec as P

R = 32
LEVELS = 4
CHUNKS = 4
ROWS = 128
PIECES = ((0, 128), (128, 128), (256, 128), (384, 64), (448, 64))
MESH = pl.DeviceIdType.MESH


def iota(shape, dim):
    return lax.broadcasted_iota(jnp.int32, shape, dim)


def order_of_stages():
    first = [(0, 0)]
    for c in range(1, CHUNKS + 1):
        first += [(0, c)] if c < CHUNKS else []
        first += [(1, i) for i, (at, _) in enumerate(PIECES) if at // ROWS == c - 1]
    return first + [(l, i) for l in (2, 3) for i in range(len(PIECES))]


def kernel(
    n_grp, n_dev, x_hbm, self_hbm, cross_hbm, pat_hbm, o_ref,
    pat_ref, xn, wn, w, q, xs, xp, part, send, near, got, send_sem, recv_sem, load_sem,
):
    grp = lax.axis_index("grp")
    dev = lax.axis_index("dev")
    boxes = xn.shape[0]
    partner = (
        (grp, dev ^ (n_dev // 2)),
        (grp, dev ^ 1),
        (grp ^ (n_grp // 2), dev),
        (grp ^ 1, dev),
    )
    barrier = pltpu.get_barrier_semaphore()
    for level in range(LEVELS):
        pl.semaphore_signal(barrier, inc=1, device_id=partner[level], device_id_type=MESH)

    row0 = pl.multiple_of(dev * boxes, boxes)
    load_x = pltpu.make_async_copy(x_hbm, xn, load_sem.at[2 * LEVELS])
    load_x.start()
    load_pat = pltpu.make_async_copy(pat_hbm, pat_ref, load_sem.at[2 * LEVELS + 1])
    load_pat.start()
    loads = []
    for level in range(LEVELS):
        pair = []
        for kind, src in enumerate((self_hbm, cross_hbm)):
            copy = pltpu.make_async_copy(
                src.at[level, pl.ds(row0, boxes)], wn.at[level, kind], load_sem.at[2 * level + kind]
            )
            copy.start()
            pair.append(copy)
        loads.append(pair)

    def exchange(level, c):
        if level == 0:
            src = xn.at[:, pl.ds(c * 256, 256)]
            dst = near.at[:, pl.ds(c * 256, 256)]
        else:
            src = send.at[level - 1, pl.ds(*PIECES[c])]
            dst = got.at[level - 1, pl.ds(*PIECES[c])]
        return pltpu.make_async_remote_copy(
            src_ref=src, dst_ref=dst,
            send_sem=send_sem.at[level, c], recv_sem=recv_sem.at[level, c],
            device_id=partner[level], device_id_type=MESH,
        )

    load_x.wait()
    pl.semaphore_wait(barrier, LEVELS)
    for c in range(CHUNKS):
        exchange(0, c).start()

    load_pat.wait()
    for level in range(LEVELS):
        row = pat_ref[level, pl.ds(dev, 1), :]
        row = jnp.concatenate([row, row + boxes], axis=1)
        q[level] = (iota((ROWS, ROWS), 0) == row).astype(jnp.float32).astype(jnp.bfloat16)

    turned = iota((256, 256), 0)
    pick = ((turned % 8) * R + turned // 8 == iota((256, 256), 1)).astype(jnp.float32).astype(jnp.bfloat16)

    def prepare(level):
        for copy in loads[level]:
            copy.wait()
        for t in range(4):
            own = wn[level, 0, :, t * 256:(t + 1) * 256]
            other = wn[level, 1, :, t * 256:(t + 1) * 256]
            stack = jnp.concatenate([own, own, other, other], axis=0)
            out = lax.dot_general(
                pick, stack, (((1,), (1,)), ((), ())), preferred_element_type=jnp.float32
            )
            w[level, 0, t] = out[:, :ROWS]
            w[level, 1, t] = out[:, ROWS:]

    def stacked(ref, c):
        return jnp.concatenate(
            [ref[:, c * 256:c * 256 + 128], ref[:, c * 256 + 128:c * 256 + 256]], axis=0
        )

    def apply(level, kind, ref, accs):
        def step(r, accs):
            ws = [w[level, kind, t, pl.ds(pl.multiple_of(r * 8, 8), 8), :] for t in range(4)]
            out = []
            for k in range(len(accs) // 4):
                x = ref[pl.ds(k * R + r, 1), :]
                out += [accs[4 * k + t] + ws[t] * x for t in range(4)]
            return tuple(out)

        return lax.fori_loop(0, R, step, tuple(accs), unroll=32)

    def self_stage(level, at, rows):
        zero = jnp.zeros((8, ROWS), jnp.float32)
        accs = apply(level, 0, xs.at[level, pl.ds(at, rows)], [zero] * (rows // 8))
        for i in range(rows // 8):
            part[level, at + i * 8:at + i * 8 + 8, :] = accs[i]

    def cross_piece(level, piece):
        at, rows = PIECES[piece]
        old = [part[level, at + i * 8:at + i * 8 + 8, :] for i in range(rows // 8)]
        accs = apply(level, 1, xp.at[pl.ds(at % ROWS, rows)], old)
        total = jnp.concatenate(accs, axis=0)
        if level < LEVELS - 1:
            total = total.astype(jnp.bfloat16)
            send[level, at:at + rows, :] = total
            exchange(level + 1, piece).start()
            xs[level + 1, at:at + rows, :] = total.astype(jnp.float32)
            if level != 1:
                self_stage(level + 1, at, rows)
        else:
            total = total.T.astype(jnp.bfloat16)
            for kh in range(2):
                lane = at // ROWS * 256 + kh * ROWS + at % ROWS
                o_ref[:, lane:lane + rows] = total[kh * boxes:(kh + 1) * boxes]

    def cross_stage(level, c):
        if level == 0:
            exchange(0, c).wait_recv()
            xp[...] = lax.dot_general(
                stacked(near, c), q[0], (((0,), (0,)), ((), ())), preferred_element_type=jnp.float32
            )
            for piece, (at, _) in enumerate(PIECES):
                if at // ROWS == c:
                    cross_piece(0, piece)
        else:
            at, rows = PIECES[c]
            if level == 2:
                self_stage(2, at, rows)
            exchange(level, c).wait_recv()
            xp[at % ROWS:at % ROWS + rows, :] = jnp.dot(
                got[level - 1, at:at + rows, :], q[level], preferred_element_type=jnp.float32
            )
            cross_piece(level, c)

    prepare(0)
    for c in range(CHUNKS):
        xs[0, c * ROWS:(c + 1) * ROWS, :] = stacked(xn, c).astype(jnp.float32).T
    for c in range(CHUNKS):
        self_stage(0, c * ROWS, ROWS)
    for level in range(1, LEVELS):
        prepare(level)
    for level, c in order_of_stages():
        cross_stage(level, c)
    for level in range(LEVELS):
        for c in range(CHUNKS if level == 0 else len(PIECES)):
            exchange(level, c).wait_send()


def shards(n_grp, n_dev, coeffs, self_blocks, cross_blocks, pattern):
    boxes, width = coeffs.shape
    bf16, f32 = jnp.bfloat16, jnp.float32
    hbm = pl.BlockSpec(memory_space=pltpu.HBM)
    vmem = pl.BlockSpec(memory_space=pltpu.VMEM)
    return pl.pallas_call(
        functools.partial(kernel, n_grp, n_dev),
        out_shape=pltpu.VMEM((boxes, width), bf16),
        in_specs=[hbm, hbm, hbm, hbm],
        out_specs=vmem,
        scratch_shapes=[
            pltpu.VMEM(pattern.shape, jnp.int32),
            pltpu.VMEM((boxes, width), bf16),
            pltpu.VMEM((LEVELS, 2, boxes, width), bf16),
            pltpu.VMEM((LEVELS, 2, 4, 256, ROWS), f32),
            pltpu.VMEM((LEVELS, ROWS, ROWS), bf16),
            pltpu.VMEM((LEVELS, CHUNKS * ROWS, ROWS), f32),
            pltpu.VMEM((ROWS, ROWS), f32),
            pltpu.VMEM((LEVELS, CHUNKS * ROWS, ROWS), f32),
            pltpu.VMEM((LEVELS - 1, CHUNKS * ROWS, ROWS), bf16),
            pltpu.VMEM((boxes, width), bf16),
            pltpu.VMEM((LEVELS - 1, CHUNKS * ROWS, ROWS), bf16),
            pltpu.SemaphoreType.DMA((LEVELS, len(PIECES))),
            pltpu.SemaphoreType.DMA((LEVELS, len(PIECES))),
            pltpu.SemaphoreType.DMA((2 * LEVELS + 2,)),
        ],
        compiler_params=pltpu.CompilerParams(
            collective_id=0, has_side_effects=True, vmem_limit_bytes=60 * 2**20
        ),
        name="butterfly",
    )(coeffs, self_blocks, cross_blocks, pattern)


def solution(mesh):
    return jax.shard_map(
        functools.partial(shards, mesh.shape["grp"], mesh.shape["dev"]),
        mesh=mesh,
        in_specs=(
            P(("grp", "dev"), None),
            P(None, "grp", None),
            P(None, "grp", None),
            P(None, "grp", None),
        ),
        out_specs=P(("grp", "dev"), None),
        check_vma=False,
    )
```

```python
import functools

import jax
import jax.numpy as jnp
from jax import lax
from jax.experimental import pallas as pl
from jax.experimental.pallas import tpu as pltpu
from jax.sharding import PartitionSpec as P

R = 32
LEVELS = 4
CHUNKS = 4
ROWS = 128
MESH = pl.DeviceIdType.MESH


def iota(shape, dim):
    return lax.broadcasted_iota(jnp.int32, shape, dim)


def order_of_stages():
    first = [(0, 0)] + [p for c in range(1, CHUNKS) for p in ((0, c), (1, c - 1))] + [(1, CHUNKS - 1)]
    return first + [(l, c) for l in (2, 3) for c in range(CHUNKS)]


def kernel(
    n_grp, n_dev, x_hbm, self_hbm, cross_hbm, pat_hbm, o_ref,
    pat_ref, xn, wn, w, q, xs, xp, part, send, near, got, send_sem, recv_sem, load_sem,
):
    grp = lax.axis_index("grp")
    dev = lax.axis_index("dev")
    boxes = xn.shape[0]
    partner = (
        (grp, dev ^ (n_dev // 2)),
        (grp, dev ^ 1),
        (grp ^ (n_grp // 2), dev),
        (grp ^ 1, dev),
    )
    barrier = pltpu.get_barrier_semaphore()
    for level in range(LEVELS):
        pl.semaphore_signal(barrier, inc=1, device_id=partner[level], device_id_type=MESH)

    row0 = pl.multiple_of(dev * boxes, boxes)
    load_x = pltpu.make_async_copy(x_hbm, xn, load_sem.at[2 * LEVELS])
    load_x.start()
    load_pat = pltpu.make_async_copy(pat_hbm, pat_ref, load_sem.at[2 * LEVELS + 1])
    load_pat.start()
    loads = []
    for level in range(LEVELS):
        pair = []
        for kind, src in enumerate((self_hbm, cross_hbm)):
            copy = pltpu.make_async_copy(
                src.at[level, pl.ds(row0, boxes)], wn.at[level, kind], load_sem.at[2 * level + kind]
            )
            copy.start()
            pair.append(copy)
        loads.append(pair)

    def exchange(level, c):
        if level == 0:
            src = x_hbm.at[:, pl.ds(c * 256, 256)]
            dst = near.at[:, pl.ds(c * 256, 256)]
        else:
            src = send.at[level - 1, c]
            dst = got.at[level - 1, c]
        return pltpu.make_async_remote_copy(
            src_ref=src, dst_ref=dst,
            send_sem=send_sem.at[level, c], recv_sem=recv_sem.at[level, c],
            device_id=partner[level], device_id_type=MESH,
        )

    pl.semaphore_wait(barrier, LEVELS)
    for c in range(CHUNKS):
        exchange(0, c).start()
    load_x.wait()

    load_pat.wait()
    for level in range(LEVELS):
        row = pat_ref[level, pl.ds(dev, 1), :]
        row = jnp.concatenate([row, row + boxes], axis=1)
        q[level] = (iota((ROWS, ROWS), 0) == row).astype(jnp.float32).astype(jnp.bfloat16)

    turned = iota((256, 256), 0)
    pick = ((turned % 8) * R + turned // 8 == iota((256, 256), 1)).astype(jnp.float32).astype(jnp.bfloat16)

    def prepare(level):
        for copy in loads[level]:
            copy.wait()
        for t in range(4):
            own = wn[level, 0, :, t * 256:(t + 1) * 256]
            other = wn[level, 1, :, t * 256:(t + 1) * 256]
            stack = jnp.concatenate([own, own, other, other], axis=0)
            out = lax.dot_general(
                pick, stack, (((1,), (1,)), ((), ())), preferred_element_type=jnp.float32
            )
            w[level, 0, t] = out[:, :ROWS]
            w[level, 1, t] = out[:, ROWS:]

    def stacked(ref, c):
        return jnp.concatenate(
            [ref[:, c * 256:c * 256 + 128], ref[:, c * 256 + 128:c * 256 + 256]], axis=0
        )

    def apply(level, kind, ref, accs):
        def step(r, accs):
            ws = [w[level, kind, t, pl.ds(pl.multiple_of(r * 8, 8), 8), :] for t in range(4)]
            out = []
            for k in range(4):
                x = ref[pl.ds(k * R + r, 1), :]
                out += [accs[4 * k + t] + ws[t] * x for t in range(4)]
            return tuple(out)

        return lax.fori_loop(0, R, step, tuple(accs), unroll=32)

    def self_stage(level, c):
        zero = jnp.zeros((8, ROWS), jnp.float32)
        accs = apply(level, 0, xs.at[level, c], [zero] * 16)
        for i in range(16):
            part[level, c, i * 8:(i + 1) * 8, :] = accs[i]

    def cross_stage(level, c):
        if level == 2:
            self_stage(2, c)
        exchange(level, c).wait_recv()
        if level == 0:
            xp[...] = lax.dot_general(
                stacked(near, c), q[0], (((0,), (0,)), ((), ())), preferred_element_type=jnp.float32
            )
        else:
            xp[...] = jnp.dot(got[level - 1, c], q[level], preferred_element_type=jnp.float32)
        accs = apply(level, 1, xp, [part[level, c, i * 8:(i + 1) * 8, :] for i in range(16)])
        total = jnp.concatenate(accs, axis=0)
        if level < LEVELS - 1:
            total = total.astype(jnp.bfloat16)
            send[level, c] = total
            exchange(level + 1, c).start()
            xs[level + 1, c] = total.astype(jnp.float32)
            if level != 1:
                self_stage(level + 1, c)
        else:
            total = total.T.astype(jnp.bfloat16)
            o_ref[:, c * 256:c * 256 + 128] = total[:boxes]
            o_ref[:, c * 256 + 128:c * 256 + 256] = total[boxes:]

    prepare(0)
    for c in range(CHUNKS):
        xs[0, c] = stacked(xn, c).astype(jnp.float32).T
    for c in range(CHUNKS):
        self_stage(0, c)
    for level in range(1, LEVELS):
        prepare(level)
    for level, c in order_of_stages():
        cross_stage(level, c)
    for level in range(LEVELS):
        for c in range(CHUNKS):
            exchange(level, c).wait_send()


def shards(n_grp, n_dev, coeffs, self_blocks, cross_blocks, pattern):
    boxes, width = coeffs.shape
    bf16, f32 = jnp.bfloat16, jnp.float32
    hbm = pl.BlockSpec(memory_space=pltpu.HBM)
    vmem = pl.BlockSpec(memory_space=pltpu.VMEM)
    return pl.pallas_call(
        functools.partial(kernel, n_grp, n_dev),
        out_shape=pltpu.VMEM((boxes, width), bf16),
        in_specs=[hbm, hbm, hbm, hbm],
        out_specs=vmem,
        scratch_shapes=[
            pltpu.VMEM(pattern.shape, jnp.int32),
            pltpu.VMEM((boxes, width), bf16),
            pltpu.VMEM((LEVELS, 2, boxes, width), bf16),
            pltpu.VMEM((LEVELS, 2, 4, 256, ROWS), f32),
            pltpu.VMEM((LEVELS, ROWS, ROWS), bf16),
            pltpu.VMEM((LEVELS, CHUNKS, ROWS, ROWS), f32),
            pltpu.VMEM((ROWS, ROWS), f32),
            pltpu.VMEM((LEVELS, CHUNKS, ROWS, ROWS), f32),
            pltpu.VMEM((LEVELS - 1, CHUNKS, ROWS, ROWS), bf16),
            pltpu.VMEM((boxes, width), bf16),
            pltpu.VMEM((LEVELS - 1, CHUNKS, ROWS, ROWS), bf16),
            pltpu.SemaphoreType.DMA((LEVELS, CHUNKS)),
            pltpu.SemaphoreType.DMA((LEVELS, CHUNKS)),
            pltpu.SemaphoreType.DMA((2 * LEVELS + 2,)),
        ],
        compiler_params=pltpu.CompilerParams(
            collective_id=0, has_side_effects=True, vmem_limit_bytes=60 * 2**20
        ),
        name="butterfly",
    )(coeffs, self_blocks, cross_blocks, pattern)


def solution(mesh):
    return jax.shard_map(
        functools.partial(shards, mesh.shape["grp"], mesh.shape["dev"]),
        mesh=mesh,
        in_specs=(
            P(("grp", "dev"), None),
            P(None, "grp", None),
            P(None, "grp", None),
            P(None, "grp", None),
        ),
        out_specs=P(("grp", "dev"), None),
        check_vma=False,
    )
```
